256 devices in a mesh: dp: 16 (over z_lo, y), mp: 16 (over z_hi, x, core).
Axes of the slice: x: 4, y: 4, z: 8 (z_hi: 2, z_lo: 4; z = z_hi * 4 + z_lo), core: 2. Of those that a mesh axis runs over, the one named last changes fastest.
Arguments:
- context: bfloat16 [8192, 6144], P('dp', 'mp'), may hold values from -6 to 6
- w_out: bfloat16 [6144, 6144], P('mp'), may hold values from -0.078125 to 0.078125
- residual: bfloat16 [8192, 6144], P(('dp', 'mp')), may hold values from -6 to 6
- gain: float32 [6144], replicated, may hold values from 0.5 to 1.5
- cotangent: bfloat16 [8192, 6144], P(('dp', 'mp')), may hold values from -6 to 6
Outputs:
- normed: bfloat16 [8192, 6144], P(('dp', 'mp'))
- residual_stream_gradient: bfloat16 [8192, 6144], P(('dp', 'mp'))
- context_grad: bfloat16 [8192, 6144], P('dp', 'mp')
- weight_grad: float32 [6144, 6144], P('mp', 'dp')
The draws below stay inside these ranges and needn't reach their ends.
All inputs are finite; a program needn't handle non-finite values.
Results may differ from the reference program's by a relative error of at most 0.015.
Values may be sent and summed in bfloat16 or wider, within the bound.
No kernel may reach another device: no remote copies, remote signals or barrier semaphores. Data moves between devices by JAX's collectives and lax.ppermute only.
A program may use at most 128 MiB of HBM per device.

```python
import math
import jax
import jax.numpy as jnp
from jax import lax

D = 6144
TOKENS = 8192
N_MP = 16


def levels(key, extent, split, low, largest):
    def one(dim, shards_of):
        draws = jax.random.uniform(jax.random.fold_in(jax.random.fold_in(key, 6), dim), (shards_of,), jnp.float32, low / len(split), largest / len(split))
        return jnp.repeat(jnp.exp(draws), extent[dim] // shards_of).reshape((-1,) + (1,) * (len(extent) - dim - 1))

    factor_of = one(*split[0])
    for cut in split[1:]:
        factor_of = factor_of * one(*cut)
    return factor_of


def gaussian(key, shape, scale, limit, split=(), dtype=jnp.bfloat16):
    result = jax.random.normal(key, shape, jnp.float32) * scale
    if len(split) > 0:
        result = levels(key, shape, split, -0.22, 0.18) * result
    return jnp.clip(result, min=-limit, max=limit).astype(dtype)


def setup_inputs(seed: int = 0) -> dict:
    arg_keys = jax.random.split(jax.random.key(seed), 6)
    return {
        "context": gaussian(arg_keys[0], (TOKENS, D), 1.0, 6.0, ((0, 16), (1, 16))),
        "w_out": gaussian(arg_keys[1], (D, D), D ** -0.5, 0.078125, ((0, 16),)),
        "residual": gaussian(arg_keys[2], (TOKENS, D), 1.0, 6.0, ((0, 256),)),
        "gain": jnp.clip(1.0 + 0.1 * jax.random.normal(arg_keys[3], (D,), jnp.float32), 0.5, 1.5),
        "cotangent": gaussian(arg_keys[4], (TOKENS, D), 1.0, 6.0, ((0, 256),)),
    }


def reference(context, w_out, residual, gain, cotangent):
    shard_width = D // N_MP
    mixed = jnp.zeros((TOKENS, D), jnp.float32)
    for column_block in range(N_MP):
        lower = column_block * shard_width
        partial_value = jnp.dot(context[:, lower:lower + shard_width], w_out[lower:lower + shard_width, :], preferred_element_type=jnp.float32)
        rounded = lax.optimization_barrier(partial_value.astype(jnp.bfloat16))
        mixed = mixed + rounded.astype(jnp.float32)
    presum = mixed + residual.astype(jnp.float32)
    average = lax.optimization_barrier(jnp.mean(presum, axis=-1, keepdims=True))
    centered_input = presum - average
    inverse_deviation = lax.rsqrt(lax.optimization_barrier(jnp.mean(centered_input * centered_input, axis=-1, keepdims=True)) + 1e-06)
    normalized_input = centered_input * inverse_deviation
    normed = (normalized_input * gain).astype(jnp.bfloat16)
    scaled_output = cotangent.astype(jnp.float32) * gain
    first_moment = lax.optimization_barrier(jnp.mean(scaled_output, axis=-1, keepdims=True))
    second_moment = lax.optimization_barrier(jnp.mean(scaled_output * normalized_input, axis=-1, keepdims=True))
    residual_stream_gradient = (inverse_deviation * (scaled_output - first_moment - normalized_input * second_moment)).astype(jnp.bfloat16)
    context_grad = lax.dot_general(residual_stream_gradient, w_out, (((1,), (1,)), ((), ())), preferred_element_type=jnp.float32).astype(jnp.bfloat16)
    weight_grad = lax.dot_general(context, residual_stream_gradient, (((0,), (0,)), ((), ())), preferred_element_type=jnp.float32)
    weight_grad = weight_grad * (1.0 / math.sqrt(TOKENS))
    return (normed, residual_stream_gradient, context_grad, weight_grad)
```

```python
import math

import jax
import jax.numpy as jnp
from jax import lax
from jax.sharding import PartitionSpec as P

F32 = jnp.float32
BF16 = jnp.bfloat16
DX = (1, 2, 3, 0)
ORDER = [(dc, dz, dx) for dc in (1, 0) for dz in (1, 0) for dx in DX]


def mp_perm(dz=0, dx=0, dc=0):
    pairs = []
    for m in range(16):
        zh, x, c = m // 8, (m // 2) % 4, m % 2
        pairs.append((m, (zh ^ dz) * 8 + ((x + dx) % 4) * 2 + (c ^ dc)))
    return pairs


def dp_perm(dz=0, dy=0):
    return [(d, ((d // 4 + dz) % 4) * 4 + (d + dy) % 4) for d in range(16)]


def to_core(a):
    return lax.ppermute(a, "mp", mp_perm(dc=1))


def to_z(a):
    return lax.ppermute(a, "mp", mp_perm(dz=1))


def to_right(a):
    return lax.ppermute(a, "mp", mp_perm(dx=1))


def to_left(a):
    return lax.ppermute(a, "mp", mp_perm(dx=3))


def add(*terms):
    total = terms[0].astype(F32)
    for t in terms[1:]:
        total = total + t.astype(F32)
    return total


def reduce_x(q):
    r = q.shape[0] // 4
    h = r // 2
    b1, b2, b3, b0 = (q[i * r : (i + 1) * r] for i in range(4))
    rp = to_right(jnp.concatenate([b1[h:], b2[:h]], axis=0))
    rm = to_left(jnp.concatenate([b3[:h], b2[h:]], axis=0))
    tp = to_right(add(b1[:h], rp[h:]).astype(BF16))
    tm = to_left(add(b3[h:], rm[h:]).astype(BF16))
    lower = add(b0[:h], rm[:h], tp)
    upper = add(b0[h:], rp[:h], tm)
    return jnp.concatenate([lower, upper], axis=0)


def gather_x(b):
    h = b.shape[0] // 2
    from_left = to_right(b)
    from_right = to_left(b)
    far_a = to_right(from_left[:h])
    far_b = to_left(from_right[h:])
    return jnp.concatenate([from_right, far_a, far_b, from_left, b], axis=0)


def gather_mp(b):
    other_z = to_z(b)
    own = gather_x(b)
    far = gather_x(other_z)
    return far, own


def turn(grad):
    r = grad.shape[0]
    me = lax.axis_index("dp")
    z, y = me // 4, me % 4
    blocks = grad.reshape(r, 16, -1).transpose(1, 0, 2)
    there = jnp.stack([((z + dz) % 4) * 4 + (y + dy) % 4 for dy in range(4) for dz in range(4)])
    send = blocks[there].reshape(4, 4, r, -1)
    held = [send[0]] + [lax.ppermute(send[dy], "dp", dp_perm(dy=dy)) for dy in (1, 2, 3)]
    held = jnp.stack(held, axis=1)
    got = [held[0]] + [lax.ppermute(held[dz], "dp", dp_perm(dz=dz)) for dz in (1, 2, 3)]
    got = jnp.stack(got).reshape(16, r, -1)
    back = jnp.stack([((z - d // 4) % 4) * 4 + (y - d % 4) % 4 for d in range(16)])
    return got[back].reshape(16 * r, -1)


def contract_rows(a, b):
    return lax.dot_general(a, b, (((0,), (0,)), ((), ())), preferred_element_type=F32)


def contract_columns(a, b):
    return lax.dot_general(a, b, (((1,), (1,)), ((), ())), preferred_element_type=F32)


def per_device(context, w_out, residual, gain, cotangent):
    rows, width = context.shape
    r = rows // 16
    half, quarter = rows // 2, rows // 4
    features = w_out.shape[1]
    row_factor = 1.0 / math.sqrt(rows * 16)
    me = lax.axis_index("mp")
    zh, x, c = me // 8, (me // 2) % 4, me % 2
    idx = jnp.stack([(zh ^ dz) * 8 + ((x + dx) % 4) * 2 + (c ^ dc) for dc, dz, dx in ORDER])
    ctx = context.reshape(16, r, width)[idx].reshape(rows, width)

    p_other = jnp.dot(ctx[:half], w_out, preferred_element_type=F32).astype(BF16)
    p_own = jnp.dot(ctx[half:], w_out, preferred_element_type=F32).astype(BF16)
    q0 = add(p_own[:quarter], to_core(p_other[:quarter])).astype(BF16)
    q1 = add(p_own[quarter:], to_core(p_other[quarter:])).astype(BF16)
    fh = features // 2
    z0 = to_z(reduce_x(q0[:, :fh]).astype(BF16))
    z1 = to_z(reduce_x(q0[:, fh:]).astype(BF16))
    mixed = reduce_x(q1) + jnp.concatenate([z0, z1], axis=1).astype(F32)

    ctx_pair = jnp.stack([ctx[half:], to_core(ctx[:half])])
    ctx_all = lax.all_gather(ctx_pair, "dp", axis=0)
    ctx_all = ctx_all.reshape(16, 2, 8, r, width).transpose(1, 2, 0, 3, 4).reshape(2, 8 * rows, width)
    w_sibling = to_core(w_out)

    presum = mixed + residual.astype(F32)
    average = jnp.mean(presum, axis=-1, keepdims=True)
    centered = presum - average
    inverse = lax.rsqrt(jnp.mean(centered * centered, axis=-1, keepdims=True) + 1e-06)
    xhat = centered * inverse
    normed = (xhat * gain).astype(BF16)
    scaled = cotangent.astype(F32) * gain
    first = jnp.mean(scaled, axis=-1, keepdims=True)
    second = jnp.mean(scaled * xhat, axis=-1, keepdims=True)
    grad = (inverse * (scaled - first - xhat * second)).astype(BF16)

    gathered = jnp.concatenate(gather_mp(grad), axis=0)
    far, own = gather_mp(turn(grad))

    cg_own = contract_columns(gathered, w_out).astype(BF16)
    cg_sibling = contract_columns(gathered, w_sibling).astype(BF16)
    cg = jnp.concatenate([to_core(cg_sibling), cg_own], axis=0)
    pos = [
        (1 - ((m % 2) ^ c)) * 8 + (1 - ((m // 8) ^ zh)) * 4 + ((m // 2) % 4 - x + 3) % 4 for m in range(16)
    ]
    context_grad = cg.reshape(16, r, width)[jnp.stack(pos)].reshape(rows, width)

    k = 4 * rows
    wg_sibling = contract_rows(ctx_all[1, :k], far) + contract_rows(ctx_all[1, k:], own)
    wg_own = contract_rows(ctx_all[0, :k], far) + contract_rows(ctx_all[0, k:], own)
    weight_grad = (wg_own + to_core(wg_sibling)) * row_factor
    return (normed, grad, context_grad, weight_grad)


def solution(mesh):
    return jax.shard_map(
        per_device,
        mesh=mesh,
        in_specs=(P("dp", "mp"), P("mp", None), P(("dp", "mp"), None), P(), P(("dp", "mp"), None)),
        out_specs=(P(("dp", "mp"), None), P(("dp", "mp"), None), P("dp", "mp"), P("mp", "dp")),
        check_vma=False,
    )
```

```python
import math

import jax
import jax.numpy as jnp
from jax import lax
from jax.experimental import pallas as pl
from jax.experimental.pallas import tpu as pltpu
from jax.sharding import PartitionSpec as P

F32 = jnp.float32
BF16 = jnp.bfloat16
DX = (1, 2, 3, 0)
ORDER = [(dz, dc, dx) for dz in (1, 0) for dc in (1, 0) for dx in DX]


def mp_perm(dz=0, dx=0, dc=0):
    pairs = []
    for m in range(16):
        zh, x, c = m // 8, (m // 2) % 4, m % 2
        pairs.append((m, (zh ^ dz) * 8 + ((x + dx) % 4) * 2 + (c ^ dc)))
    return pairs


def to_core(a):
    return lax.ppermute(a, "mp", mp_perm(dc=1))


def to_z(a):
    return lax.ppermute(a, "mp", mp_perm(dz=1))


def to_x(a, dx):
    return lax.ppermute(a, "mp", mp_perm(dx=dx))


def add(*terms):
    total = terms[0].astype(F32)
    for t in terms[1:]:
        total = total + t.astype(F32)
    return total


def project_kernel(a_ref, w_ref, other_ref, own_ref):
    n = other_ref.shape[0]
    out = jnp.dot(a_ref[...], w_ref[...], preferred_element_type=F32).astype(BF16)
    other_ref[...] = out[:n]
    own_ref[...] = out[n:]


def project(a, w):
    rows, width = a.shape
    features = w.shape[1]
    tile = min(1024, features)
    half = jax.ShapeDtypeStruct((rows // 2, features), BF16)
    out_spec = pl.BlockSpec((rows // 2, tile), lambda i: (0, i))
    return pl.pallas_call(
        project_kernel,
        grid=(features // tile,),
        in_specs=[pl.BlockSpec((rows, width), lambda i: (0, 0)), pl.BlockSpec((width, tile), lambda i: (0, i))],
        out_specs=[out_spec, out_spec],
        out_shape=[half, half],
        cost_estimate=pl.CostEstimate(
            flops=2 * rows * width * features, bytes_accessed=2 * features * (rows + width), transcendentals=0
        ),
    )(a, w)


def reduce_x(q):
    r = q.shape[0] // 4
    b1, b2, b3, b0 = (q[i * r : (i + 1) * r] for i in range(4))
    return add(b0, to_x(b1, 1), to_x(b2, 2), to_x(b3, 3))


def gather_x(b):
    return [to_x(b, 3), to_x(b, 2), to_x(b, 1), b]


def contract_rows(a, b):
    return lax.dot_general(a, b, (((0,), (0,)), ((), ())), preferred_element_type=F32)


def contract_columns(a, b):
    return lax.dot_general(a, b, (((1,), (1,)), ((), ())), preferred_element_type=F32)


def by_image(blocks):
    r = blocks[0].shape[0] // 16
    parts = [b.reshape(16, r, -1) for b in blocks]
    return jnp.concatenate(parts, axis=1).reshape(16 * r * len(blocks), -1)


def per_device(context, w_out, residual, gain, cotangent):
    rows, width = context.shape
    r, quarter = rows // 16, rows // 4
    row_factor = 1.0 / math.sqrt(rows * 16)
    me = lax.axis_index("mp")
    zh, x, c = me // 8, (me // 2) % 4, me % 2
    idx = jnp.stack([(zh ^ dz) * 8 + ((x + dx) % 4) * 2 + (c ^ dc) for dz, dc, dx in ORDER])
    ctx = context.reshape(16, r, width)[idx].reshape(4, quarter, width)

    other0, own0 = project(ctx[:2].reshape(2 * quarter, width), w_out)
    q0 = add(own0, to_core(other0)).astype(BF16)
    other1, own1 = project(ctx[2:].reshape(2 * quarter, width), w_out)
    q1 = add(own1, to_core(other1)).astype(BF16)
    z0 = to_z(reduce_x(q0).astype(BF16))
    mixed = reduce_x(q1)

    there = to_core(ctx[::2].reshape(2 * quarter, width))
    ctx_far = lax.all_gather(jnp.concatenate([ctx[1], there[:quarter]], axis=1), "dp", axis=0, tiled=True)
    ctx_near = lax.all_gather(jnp.concatenate([ctx[3], there[quarter:]], axis=1), "dp", axis=0, tiled=True)
    w_sibling = to_core(w_out)

    presum = mixed + z0.astype(F32) + residual.astype(F32)
    average = jnp.mean(presum, axis=-1, keepdims=True)
    centered = presum - average
    inverse = lax.rsqrt(jnp.mean(centered * centered, axis=-1, keepdims=True) + 1e-06)
    xhat = centered * inverse
    normed = (xhat * gain).astype(BF16)
    scaled = cotangent.astype(F32) * gain
    first = jnp.mean(scaled, axis=-1, keepdims=True)
    second = jnp.mean(scaled * xhat, axis=-1, keepdims=True)
    grad = (inverse * (scaled - first - xhat * second)).astype(BF16)

    near = gather_x(grad)
    far = gather_x(to_z(grad))
    blocks = grad.reshape(r, 16, width).transpose(1, 0, 2).reshape(rows, width)
    turned = lax.all_to_all(blocks, "dp", 0, 0, tiled=True)
    turned_near = gather_x(turned)
    turned_far = gather_x(to_z(turned))

    gathered = jnp.concatenate(far + near, axis=0)
    cg_own = contract_columns(gathered, w_out).astype(BF16)
    cg_sibling = contract_columns(gathered, w_sibling).astype(BF16)
    cg = jnp.concatenate([to_core(cg_sibling), cg_own], axis=0)
    pos = [
        (1 - ((m % 2) ^ c)) * 8 + (1 - ((m // 8) ^ zh)) * 4 + ((m // 2) % 4 - x + 3) % 4 for m in range(16)
    ]
    context_grad = cg.reshape(16, r, width)[jnp.stack(pos)].reshape(rows, width)

    wg_near = contract_rows(ctx_near, by_image(turned_near))
    turned_far, wg_near, context_grad = lax.optimization_barrier((turned_far, wg_near, context_grad))
    wg = wg_near + contract_rows(ctx_far, by_image(turned_far))
    weight_grad = (wg[:width] + to_core(wg[width:])) * row_factor
    return (normed, grad, context_grad, weight_grad)


def solution(mesh):
    return jax.shard_map(
        per_device,
        mesh=mesh,
        in_specs=(P("dp", "mp"), P("mp", None), P(("dp", "mp"), None), P(), P(("dp", "mp"), None)),
        out_specs=(P(("dp", "mp"), None), P(("dp", "mp"), None), P("dp", "mp"), P("mp", "dp")),
        check_vma=False,
    )
```

```python
import math

import jax
import jax.numpy as jnp
from jax import lax
from jax.experimental import pallas as pl
from jax.experimental.pallas import tpu as pltpu
from jax.sharding import PartitionSpec as P

F32 = jnp.float32
BF16 = jnp.bfloat16
DX = (1, 2, 3, 0)
ORDER = [(dz, dc, dx) for dz in (1, 0) for dc in (1, 0) for dx in DX]


def mp_perm(dz=0, dx=0, dc=0):
    pairs = []
    for m in range(16):
        zh, x, c = m // 8, (m // 2) % 4, m % 2
        pairs.append((m, (zh ^ dz) * 8 + ((x + dx) % 4) * 2 + (c ^ dc)))
    return pairs


def to_core(a):
    return lax.ppermute(a, "mp", mp_perm(dc=1))


def to_z(a):
    return lax.ppermute(a, "mp", mp_perm(dz=1))


def to_x(a, dx):
    return lax.ppermute(a, "mp", mp_perm(dx=dx))


def add(*terms):
    total = terms[0].astype(F32)
    for t in terms[1:]:
        total = total + t.astype(F32)
    return total


def project_kernel(a_ref, w_ref, other_ref, own_ref):
    n = other_ref.shape[0]
    out = jnp.dot(a_ref[...], w_ref[...], preferred_element_type=F32).astype(BF16)
    other_ref[...] = out[:n]
    own_ref[...] = out[n:]


def project(a, w):
    rows, width = a.shape
    features = w.shape[1]
    tile = min(1024, features)
    half = jax.ShapeDtypeStruct((rows // 2, features), BF16)
    out_spec = pl.BlockSpec((rows // 2, tile), lambda i: (0, i))
    return pl.pallas_call(
        project_kernel,
        grid=(features // tile,),
        in_specs=[pl.BlockSpec((rows, width), lambda i: (0, 0)), pl.BlockSpec((width, tile), lambda i: (0, i))],
        out_specs=[out_spec, out_spec],
        out_shape=[half, half],
        cost_estimate=pl.CostEstimate(
            flops=2 * rows * width * features, bytes_accessed=2 * features * (rows + width), transcendentals=0
        ),
    )(a, w)


def send_x(q):
    r = q.shape[0] // 4
    b1, b2, b3, b0 = (q[i * r : (i + 1) * r] for i in range(4))
    return [b0, to_x(b1, 1), to_x(b2, 2), to_x(b3, 3)]


def after(*values):
    return lax.optimization_barrier(values)


def gather_x(b):
    return [to_x(b, 3), to_x(b, 2), to_x(b, 1), b]


def contract_rows(a, b):
    return lax.dot_general(a, b, (((0,), (0,)), ((), ())), preferred_element_type=F32)


def contract_columns(a, b):
    return lax.dot_general(a, b, (((1,), (1,)), ((), ())), preferred_element_type=F32)


def by_image(blocks):
    r = blocks[0].shape[0] // 16
    parts = [b.reshape(16, r, -1) for b in blocks]
    return jnp.concatenate(parts, axis=1).reshape(16 * r * len(blocks), -1)


def per_device(context, w_out, residual, gain, cotangent):
    rows, width = context.shape
    r, quarter = rows // 16, rows // 4
    row_factor = 1.0 / math.sqrt(rows * 16)
    me = lax.axis_index("mp")
    zh, x, c = me // 8, (me // 2) % 4, me % 2
    idx = jnp.stack([(zh ^ dz) * 8 + ((x + dx) % 4) * 2 + (c ^ dc) for dz, dc, dx in ORDER])
    ctx = context.reshape(16, r, width)[idx].reshape(4, quarter, width)

    other0, own0 = project(ctx[:2].reshape(2 * quarter, width), w_out)
    there = to_core(ctx[::2].reshape(2 * quarter, width))
    from0 = to_core(other0)
    ctx_low, from0, there = after(ctx[2:], from0, there)
    sent0 = send_x(add(own0, from0).astype(BF16))
    other1, own1 = project(ctx_low.reshape(2 * quarter, width), w_out)
    q1 = add(own1, to_core(other1)).astype(BF16)
    q1, *sent0 = after(q1, *sent0)
    z0 = to_z(add(*sent0).astype(BF16))
    sent1 = send_x(q1)

    pair = jnp.concatenate([ctx[1::2].reshape(2 * quarter, width), there], axis=1)
    ctx_all = lax.all_gather(pair, "dp", axis=0)
    w_sibling = to_core(w_out)
    z0, w_sibling, *sent1 = after(z0, w_sibling, *sent1)
    mixed = add(*sent1)

    presum = mixed + z0.astype(F32) + residual.astype(F32)
    average = jnp.mean(presum, axis=-1, keepdims=True)
    centered = presum - average
    inverse = lax.rsqrt(jnp.mean(centered * centered, axis=-1, keepdims=True) + 1e-06)
    xhat = centered * inverse
    normed = (xhat * gain).astype(BF16)
    scaled = cotangent.astype(F32) * gain
    first = jnp.mean(scaled, axis=-1, keepdims=True)
    second = jnp.mean(scaled * xhat, axis=-1, keepdims=True)
    grad = (inverse * (scaled - first - xhat * second)).astype(BF16)

    far0 = to_z(grad)
    near = gather_x(grad)
    near_g, far0 = after(near, far0)
    blocks = near_g[3].reshape(r, 16, width).transpose(1, 0, 2).reshape(rows, width)
    turned = lax.all_to_all(blocks, "dp", 0, 0, tiled=True)
    far = gather_x(far0)
    turned, far = after(turned, far)
    turned_far0 = to_z(turned)
    turned_near = gather_x(turned)
    turned_near, turned_far0, ctx_all = after(turned_near, turned_far0, ctx_all)
    turned_far = gather_x(turned_far0)

    gathered = jnp.concatenate(far + near_g, axis=0)
    cg_own = contract_columns(gathered, w_out).astype(BF16)
    cg_sibling = contract_columns(gathered, w_sibling).astype(BF16)
    cg = jnp.concatenate([to_core(cg_sibling), cg_own], axis=0)
    pos = [
        (1 - ((m % 2) ^ c)) * 8 + (1 - ((m // 8) ^ zh)) * 4 + ((m // 2) % 4 - x + 3) % 4 for m in range(16)
    ]
    context_grad = cg.reshape(16, r, width)[jnp.stack(pos)].reshape(rows, width)

    ctx_far = ctx_all[:, :quarter].reshape(16 * quarter, 2 * width)
    ctx_near = ctx_all[:, quarter:].reshape(16 * quarter, 2 * width)
    wg_near = contract_rows(ctx_near, by_image(turned_near))
    turned_far, wg_near, ctx_far, context_grad = after(turned_far, wg_near, ctx_far, context_grad)
    wg = wg_near + contract_rows(ctx_far, by_image(turned_far))
    weight_grad = (wg[:width] + to_core(wg[width:])) * row_factor
    return (normed, grad, context_grad, weight_grad)


def solution(mesh):
    return jax.shard_map(
        per_device,
        mesh=mesh,
        in_specs=(P("dp", "mp"), P("mp", None), P(("dp", "mp"), None), P(), P(("dp", "mp"), None)),
        out_specs=(P(("dp", "mp"), None), P(("dp", "mp"), None), P("dp", "mp"), P("mp", "dp")),
        check_vma=False,
    )
```

```python
import math

import jax
import jax.numpy as jnp
from jax import lax
from jax.experimental import pallas as pl
from jax.experimental.pallas import tpu as pltpu
from jax.sharding import PartitionSpec as P

F32 = jnp.float32
BF16 = jnp.bfloat16
DX = (1, 2, 3, 0)
ORDER = [(dz, dc, dx) for dz in (1, 0) for dc in (1, 0) for dx in DX]

GROUPS_Y = [[4 * z + y for y in range(4)] for z in range(4)]
Y_THEN_Z = [[4 * z + y for y in range(4) for z in range(4)]]


def mp_perm(dz=0, dx=0, dc=0):
    pairs = []
    for m in range(16):
        zh, x, c = m // 8, (m // 2) % 4, m % 2
        pairs.append((m, (zh ^ dz) * 8 + ((x + dx) % 4) * 2 + (c ^ dc)))
    return pairs


def dp_swap(dz):
    return [(d, d ^ (4 * dz)) for d in range(16)]


def to_core(a):
    return lax.ppermute(a, "mp", mp_perm(dc=1))


def to_z(a):
    return lax.ppermute(a, "mp", mp_perm(dz=1))


def to_x(a, dx):
    return lax.ppermute(a, "mp", mp_perm(dx=dx))


def add(*terms):
    total = terms[0].astype(F32)
    for t in terms[1:]:
        total = total + t.astype(F32)
    return total


def project_kernel(a_ref, w_ref, other_ref, own_ref):
    n = other_ref.shape[0]
    out = jnp.dot(a_ref[...], w_ref[...], preferred_element_type=F32).astype(BF16)
    other_ref[...] = out[:n]
    own_ref[...] = out[n:]


def project(a, w):
    rows, width = a.shape
    features = w.shape[1]
    tile = min(2048, features)
    half = jax.ShapeDtypeStruct((rows // 2, features), BF16)
    out_spec = pl.BlockSpec((rows // 2, tile), lambda i: (0, i))
    return pl.pallas_call(
        project_kernel,
        grid=(features // tile,),
        in_specs=[pl.BlockSpec((rows, width), lambda i: (0, 0)), pl.BlockSpec((width, tile), lambda i: (0, i))],
        out_specs=[out_spec, out_spec],
        out_shape=[half, half],
        compiler_params=pltpu.CompilerParams(vmem_limit_bytes=24 * 2**20),
        cost_estimate=pl.CostEstimate(
            flops=2 * rows * width * features, bytes_accessed=2 * features * (rows + width), transcendentals=0
        ),
    )(a, w)


def send_x(q):
    r = q.shape[0] // 4
    b1, b2, b3, b0 = (q[i * r : (i + 1) * r] for i in range(4))
    return [b0, to_x(b1, 1), to_x(b2, 2), to_x(b3, 3)]


def after(*values):
    return lax.optimization_barrier(values)


def gather_x(b):
    return [to_x(b, 3), to_x(b, 2), to_x(b, 1), b]


def spread_z(v, order):
    four = jnp.concatenate([v, lax.ppermute(v, "dp", dp_swap(2))])
    return four[order].reshape(-1, v.shape[-1])


def gather_y(v):
    return lax.all_gather(v, "dp", axis=0, axis_index_groups=GROUPS_Y, tiled=True)


def contract_rows(a, b):
    return lax.dot_general(a, b, (((0,), (0,)), ((), ())), preferred_element_type=F32)


def back_project_kernel(*refs):
    blocks, (w_ref, v_ref, own_ref, sibling_ref, rows_ref, total_ref) = refs[:-6], refs[-6:]
    r = blocks[0].shape[0]
    width = w_ref.shape[0]
    step = pl.program_id(0)

    @pl.when(step == 0)
    def _():
        total_ref[...] = jnp.zeros_like(total_ref)

    for k, b in enumerate(blocks):
        rows_ref[k * r : (k + 1) * r] = b[...]
    rows = rows_ref[...]
    for k, w in enumerate((w_ref, v_ref)):
        total_ref[k] += lax.dot_general(rows, w[...], (((1,), (1,)), ((), ())), preferred_element_type=F32)

    @pl.when(step == pl.num_programs(0) - 1)
    def _():
        own_ref[...] = total_ref[0].astype(BF16)
        sibling_ref[...] = total_ref[1].astype(BF16)


def back_project(blocks, w, v):
    r, features = blocks[0].shape
    rows, width = r * len(blocks), w.shape[0]
    tile = min(2048, features)
    out = jax.ShapeDtypeStruct((rows, width), BF16)
    whole = pl.BlockSpec((rows, width), lambda i: (0, 0))
    block = pl.BlockSpec((r, tile), lambda i: (0, i))
    weight = pl.BlockSpec((width, tile), lambda i: (0, i))
    return pl.pallas_call(
        back_project_kernel,
        grid=(features // tile,),
        in_specs=[block] * len(blocks) + [weight, weight],
        out_specs=[whole, whole],
        out_shape=[out, out],
        scratch_shapes=[pltpu.VMEM((rows, tile), BF16), pltpu.VMEM((2, rows, width), F32)],
        compiler_params=pltpu.CompilerParams(vmem_limit_bytes=24 * 2**20),
        cost_estimate=pl.CostEstimate(
            flops=4 * rows * width * features, bytes_accessed=2 * features * (rows + 2 * width), transcendentals=0
        ),
    )(*blocks, w, v)


def by_image(blocks):
    r = blocks[0].shape[0] // 16
    parts = [b.reshape(16, r, -1) for b in blocks]
    return jnp.concatenate(parts, axis=1).reshape(16 * r * len(blocks), -1)


def per_device(context, w_out, residual, gain, cotangent):
    rows, width = context.shape
    r, quarter = rows // 16, rows // 4
    row_factor = 1.0 / math.sqrt(rows * 16)
    me = lax.axis_index("mp")
    zh, x, c = me // 8, (me // 2) % 4, me % 2
    idx = jnp.stack([(zh ^ dz) * 8 + ((x + dx) % 4) * 2 + (c ^ dc) for dz, dc, dx in ORDER])
    ctx = context.reshape(16, r, width)[idx].reshape(4, quarter, width)

    there = to_core(ctx[::2])
    other0, own0 = project(ctx[:2].reshape(2 * quarter, width), w_out)
    other0, there = after(other0, there)
    from0 = to_core(other0)
    pair = jnp.concatenate([ctx[1::2], there], axis=-1)
    two = jnp.stack([pair, lax.ppermute(pair, "dp", dp_swap(1))])
    order_z = (lax.axis_index("dp") // 4) ^ jnp.arange(4)
    near_z = spread_z(two[:, 1], order_z)
    ctx_low, from0 = after(ctx[2:], from0)
    sent0 = send_x(add(own0, from0).astype(BF16))
    other1, own1 = project(ctx_low.reshape(2 * quarter, width), w_out)
    q1 = add(own1, to_core(other1)).astype(BF16)
    z0 = add(*sent0).astype(BF16)
    z0, q1 = after(z0, q1)
    z0 = to_z(z0)
    sent1 = send_x(q1)
    z0, near_z, *sent1 = after(z0, near_z, *sent1)
    ctx_near = gather_y(near_z)
    mixed = add(*sent1)

    presum = mixed + z0.astype(F32) + residual.astype(F32)
    average = jnp.mean(presum, axis=-1, keepdims=True)
    centered = presum - average
    inverse = lax.rsqrt(jnp.mean(centered * centered, axis=-1, keepdims=True) + 1e-06)
    xhat = centered * inverse
    normed = (xhat * gain).astype(BF16)
    scaled = cotangent.astype(F32) * gain
    first = jnp.mean(scaled, axis=-1, keepdims=True)
    second = jnp.mean(scaled * xhat, axis=-1, keepdims=True)
    grad = (inverse * (scaled - first - xhat * second)).astype(BF16)

    grad, w_there = after(grad, w_out)
    w_sibling = to_core(w_there)
    far0 = to_z(grad)
    near = gather_x(grad)
    far_z = two[:, 0]
    far0, far_z, w_sibling, *near = after(far0, far_z, w_sibling, *near)
    blocks = near[3].reshape(r, 4, 4, width).transpose(2, 1, 0, 3).reshape(rows, width)
    turned = lax.all_to_all(blocks, "dp", 0, 0, axis_index_groups=Y_THEN_Z, tiled=True)
    far_z = spread_z(far_z, order_z)
    far = gather_x(far0)
    turned, far_z, *far = after(turned, far_z, *far)
    ctx_far = gather_y(far_z)
    turned_far0 = to_z(turned)
    turned_near = gather_x(turned)
    cg_own, cg_sibling = back_project(far + near, w_out, w_sibling)
    turned_far0, cg_own, cg_sibling, *turned_near = after(turned_far0, cg_own, cg_sibling, *turned_near)
    turned_far = gather_x(turned_far0)
    cg = jnp.concatenate([to_core(cg_sibling), cg_own], axis=0)
    pos = [
        (1 - ((m % 2) ^ c)) * 8 + (1 - ((m // 8) ^ zh)) * 4 + ((m // 2) % 4 - x + 3) % 4 for m in range(16)
    ]
    context_grad = cg.reshape(16, r, width)[jnp.stack(pos)].reshape(rows, width)

    wg_near = contract_rows(ctx_near, by_image(turned_near))
    turned_far, wg_near, context_grad = after(turned_far, wg_near, context_grad)
    wg = wg_near + contract_rows(ctx_far, by_image(turned_far))
    weight_grad = (wg[:width] + to_core(wg[width:])) * row_factor
    return (normed, grad, context_grad, weight_grad)


def solution(mesh):
    return jax.shard_map(
        per_device,
        mesh=mesh,
        in_specs=(P("dp", "mp"), P("mp", None), P(("dp", "mp"), None), P(), P(("dp", "mp"), None)),
        out_specs=(P(("dp", "mp"), None), P(("dp", "mp"), None), P("dp", "mp"), P("mp", "dp")),
        check_vma=False,
    )
```

```python
import math

import jax
import jax.numpy as jnp
from jax import lax
from jax.experimental import pallas as pl
from jax.experimental.pallas import tpu as pltpu
from jax.sharding import PartitionSpec as P

F32 = jnp.float32
BF16 = jnp.bfloat16
DX = (1, 2, 3, 0)
ORDER = [(dz, dc, dx) for dz in (1, 0) for dc in (1, 0) for dx in DX]

GROUPS_Y = [[4 * z + y for y in range(4)] for z in range(4)]
Y_THEN_Z = [[4 * z + y for y in range(4) for z in range(4)]]


def mp_perm(dz=0, dx=0, dc=0):
    pairs = []
    for m in range(16):
        zh, x, c = m // 8, (m // 2) % 4, m % 2
        pairs.append((m, (zh ^ dz) * 8 + ((x + dx) % 4) * 2 + (c ^ dc)))
    return pairs


def dp_swap(dz):
    return [(d, d ^ (4 * dz)) for d in range(16)]


def to_core(a):
    return lax.ppermute(a, "mp", mp_perm(dc=1))


def to_z(a):
    return lax.ppermute(a, "mp", mp_perm(dz=1))


def to_x(a, dx):
    return lax.ppermute(a, "mp", mp_perm(dx=dx))


def add(*terms):
    total = terms[0].astype(F32)
    for t in terms[1:]:
        total = total + t.astype(F32)
    return total


def project_kernel(a_ref, w_ref, other_ref, own_ref):
    n = other_ref.shape[0]
    out = jnp.dot(a_ref[...], w_ref[...], preferred_element_type=F32).astype(BF16)
    other_ref[...] = out[:n]
    own_ref[...] = out[n:]


def project(a, w):
    rows, width = a.shape
    features = w.shape[1]
    tile = min(2048, features)
    half = jax.ShapeDtypeStruct((rows // 2, features), BF16)
    out_spec = pl.BlockSpec((rows // 2, tile), lambda i: (0, i))
    return pl.pallas_call(
        project_kernel,
        grid=(features // tile,),
        in_specs=[pl.BlockSpec((rows, width), lambda i: (0, 0)), pl.BlockSpec((width, tile), lambda i: (0, i))],
        out_specs=[out_spec, out_spec],
        out_shape=[half, half],
        compiler_params=pltpu.CompilerParams(vmem_limit_bytes=24 * 2**20),
        cost_estimate=pl.CostEstimate(
            flops=2 * rows * width * features, bytes_accessed=2 * features * (rows + width), transcendentals=0
        ),
    )(a, w)


def send_x(q):
    r = q.shape[0] // 4
    b1, b2, b3, b0 = (q[i * r : (i + 1) * r] for i in range(4))
    return [b0, to_x(b1, 1), to_x(b2, 2), to_x(b3, 3)]


def after(*values):
    return lax.optimization_barrier(values)


def gather_x(b):
    return [to_x(b, 3), to_x(b, 2), to_x(b, 1), b]


def spread_z(v):
    four = jnp.concatenate([v, lax.ppermute(v, "dp", dp_swap(2))])
    return four.reshape(-1, v.shape[-1])


def gather_y(v):
    return lax.all_gather(v, "dp", axis=0, axis_index_groups=GROUPS_Y, tiled=True)


def contract_rows(a, b):
    return lax.dot_general(a, b, (((0,), (0,)), ((), ())), preferred_element_type=F32)


def back_project_kernel(*refs):
    blocks, (w_ref, v_ref, own_ref, sibling_ref, rows_ref, total_ref) = refs[:-6], refs[-6:]
    r = blocks[0].shape[0]
    width = w_ref.shape[0]
    step = pl.program_id(0)

    @pl.when(step == 0)
    def _():
        total_ref[...] = jnp.zeros_like(total_ref)

    for k, b in enumerate(blocks):
        rows_ref[k * r : (k + 1) * r] = b[...]
    rows = rows_ref[...]
    for k, w in enumerate((w_ref, v_ref)):
        total_ref[k] += lax.dot_general(rows, w[...], (((1,), (1,)), ((), ())), preferred_element_type=F32)

    @pl.when(step == pl.num_programs(0) - 1)
    def _():
        own_ref[...] = total_ref[0].astype(BF16)
        sibling_ref[...] = total_ref[1].astype(BF16)


def back_project(blocks, w, v):
    r, features = blocks[0].shape
    rows, width = r * len(blocks), w.shape[0]
    tile = min(2048, features)
    out = jax.ShapeDtypeStruct((rows, width), BF16)
    whole = pl.BlockSpec((rows, width), lambda i: (0, 0))
    block = pl.BlockSpec((r, tile), lambda i: (0, i))
    weight = pl.BlockSpec((width, tile), lambda i: (0, i))
    return pl.pallas_call(
        back_project_kernel,
        grid=(features // tile,),
        in_specs=[block] * len(blocks) + [weight, weight],
        out_specs=[whole, whole],
        out_shape=[out, out],
        scratch_shapes=[pltpu.VMEM((rows, tile), BF16), pltpu.VMEM((2, rows, width), F32)],
        compiler_params=pltpu.CompilerParams(vmem_limit_bytes=24 * 2**20),
        cost_estimate=pl.CostEstimate(
            flops=4 * rows * width * features, bytes_accessed=2 * features * (rows + 2 * width), transcendentals=0
        ),
    )(*blocks, w, v)


def by_image(blocks):
    r = blocks[0].shape[0] // 16
    parts = [b.reshape(16, r, -1) for b in blocks]
    return jnp.concatenate(parts, axis=1).reshape(16 * r * len(blocks), -1)


def per_device(context, w_out, residual, gain, cotangent):
    rows, width = context.shape
    r, quarter = rows // 16, rows // 4
    row_factor = 1.0 / math.sqrt(rows * 16)
    me = lax.axis_index("mp")
    zh, x, c = me // 8, (me // 2) % 4, me % 2
    idx = jnp.stack([(zh ^ dz) * 8 + ((x + dx) % 4) * 2 + (c ^ dc) for dz, dc, dx in ORDER])
    ctx = context.reshape(16, r, width)[idx].reshape(4, quarter, width)

    there = to_core(ctx[::2])
    other0, own0 = project(ctx[:2].reshape(2 * quarter, width), w_out)
    other0, there = after(other0, there)
    from0 = to_core(other0)
    pair = jnp.concatenate([ctx[1::2], there], axis=-1)
    two = jnp.stack([pair, lax.ppermute(pair, "dp", dp_swap(1))])
    order_z = (lax.axis_index("dp") // 4) ^ jnp.arange(4)
    near_z = spread_z(two[:, 1])
    ctx_low, from0 = after(ctx[2:], from0)
    sent0 = send_x(add(own0, from0).astype(BF16))
    other1, own1 = project(ctx_low.reshape(2 * quarter, width), w_out)
    q1 = add(own1, to_core(other1)).astype(BF16)
    z0 = add(*sent0).astype(BF16)
    z0, q1 = after(z0, q1)
    z0 = to_z(z0)
    sent1 = send_x(q1)
    z0, near_z, *sent1 = after(z0, near_z, *sent1)
    ctx_near = gather_y(near_z)
    mixed = add(*sent1)

    presum = mixed + z0.astype(F32) + residual.astype(F32)
    average = jnp.mean(presum, axis=-1, keepdims=True)
    centered = presum - average
    inverse = lax.rsqrt(jnp.mean(centered * centered, axis=-1, keepdims=True) + 1e-06)
    xhat = centered * inverse
    normed = (xhat * gain).astype(BF16)
    scaled = cotangent.astype(F32) * gain
    first = jnp.mean(scaled, axis=-1, keepdims=True)
    second = jnp.mean(scaled * xhat, axis=-1, keepdims=True)
    grad = (inverse * (scaled - first - xhat * second)).astype(BF16)

    grad, w_there = after(grad, w_out)
    w_sibling = to_core(w_there)
    far0 = to_z(grad)
    near = gather_x(grad)
    far_z = two[:, 0]
    far0, far_z, w_sibling, *near = after(far0, far_z, w_sibling, *near)
    blocks = near[3].reshape(r, 4, 4, width).transpose(2, 1, 0, 3).reshape(rows, width)
    turned = lax.all_to_all(blocks, "dp", 0, 0, axis_index_groups=Y_THEN_Z, tiled=True)
    turned = turned.reshape(4, 4, r, width)[:, order_z].reshape(rows, width)
    far_z = spread_z(far_z)
    far = gather_x(far0)
    turned, far_z, *far = after(turned, far_z, *far)
    ctx_far = gather_y(far_z)
    turned_far0 = to_z(turned)
    turned_near = gather_x(turned)
    cg_own, cg_sibling = back_project(far + near, w_out, w_sibling)
    turned_far0, cg_own, cg_sibling, *turned_near = after(turned_far0, cg_own, cg_sibling, *turned_near)
    turned_far = gather_x(turned_far0)
    cg = jnp.concatenate([to_core(cg_sibling), cg_own], axis=0)
    pos = [
        (1 - ((m % 2) ^ c)) * 8 + (1 - ((m // 8) ^ zh)) * 4 + ((m // 2) % 4 - x + 3) % 4 for m in range(16)
    ]
    context_grad = cg.reshape(16, r, width)[jnp.stack(pos)].reshape(rows, width)

    wg_near = contract_rows(ctx_near, by_image(turned_near))
    turned_far, wg_near, context_grad = after(turned_far, wg_near, context_grad)
    wg = wg_near + contract_rows(ctx_far, by_image(turned_far))
    weight_grad = (wg[:width] + to_core(wg[width:])) * row_factor
    return (normed, grad, context_grad, weight_grad)


def solution(mesh):
    return jax.shard_map(
        per_device,
        mesh=mesh,
        in_specs=(P("dp", "mp"), P("mp", None), P(("dp", "mp"), None), P(), P(("dp", "mp"), None)),
        out_specs=(P(("dp", "mp"), None), P(("dp", "mp"), None), P("dp", "mp"), P("mp", "dp")),
        check_vma=False,
    )
```
